32 devices in a mesh: wide: 8 (over y, x, core), narrow: 4 (over z).
Axes of the slice: x: 2, y: 2, z: 4, core: 2. Of those that a mesh axis runs over, the one named last changes fastest.
Arguments:
- gcm_state: float32 [1024, 144], P('wide'), may hold values from -6 to 6
- crm_state: bfloat16 [2, 60, 256, 1024], P(None, None, 'narrow', 'wide'), may hold values from -6 to 6
- courant: float32 [60, 1024], P(None, 'wide'), may hold values from 0.1 to 0.6
- cloud_mask: int32 [60, 1024], P(None, 'wide'), may hold values 0 or 1
- level_down: float32 [60, 72], replicated, may hold values from -0.75 to 0.75
- level_up: float32 [72, 60], replicated, may hold values from -0.75 to 0.75
- column_map: int32 [1024], replicated, may hold values from 0 to 1023, as said below
Outputs:
- gcm_tendency: bfloat16 [1024, 144], P('wide')
- crm_new: bfloat16 [2, 60, 256, 1024], P(None, None, 'narrow', 'wide')
The draws below stay inside these ranges and needn't reach their ends.
Inputs may be any that keep to these rules, and one draw needn't show every extreme that they name: column_map is a bijection onto 0 to 1023; the columns of one index of wide go to at most 32 slots of any one owner, and to exactly 32 slots of half of the owners.
All inputs are finite; a program needn't handle non-finite values. No bound on the sum of `cloud_mask` on one device may be relied on, other than what follows from the above.
Results may differ from the reference program's by a relative error of at most 0.0048.
Values may be sent and summed in bfloat16 or wider, within the bound.
A program may use at most 64 MiB of HBM per device.

```python
import jax
import jax.numpy as jnp
from jax import lax

LEV = 72
CLEV = 60
CX = 256
SUB = 4
COLS_DEV = 128
NCOL = 1024
CAP = 32
N_WIDE = 8


def draw_column_map(key, part):
    rounds = N_WIDE // 2
    key_offsets = jax.random.fold_in(key, 11)
    key_places = jax.random.fold_in(key, 12)
    key_slots = jax.random.fold_in(key, 13)
    shuffled = jax.random.permutation(key_offsets, N_WIDE).astype(jnp.int32)
    rank_of = jnp.argsort(shuffled).astype(jnp.int32)
    values_all = jnp.arange(N_WIDE, dtype=jnp.int32)
    score = jnp.where(values_all == 1, -3, jnp.where(values_all == N_WIDE // 2, -2, jnp.where(values_all == N_WIDE - 1, -1, rank_of)))
    offsets = jnp.argsort(score)[:rounds].astype(jnp.int32)
    places = jax.vmap(lambda sub_key: jax.random.permutation(sub_key, COLS_DEV))(jax.random.split(key_places, N_WIDE)).astype(jnp.int32)
    slot_orders = jax.vmap(lambda sub_key: jax.random.permutation(sub_key, COLS_DEV))(jax.random.split(key_slots, N_WIDE)).astype(jnp.int32)
    source = jnp.arange(N_WIDE, dtype=jnp.int32)[:, None, None]
    round_index = jnp.arange(rounds, dtype=jnp.int32)[None, :, None]
    within = jnp.arange(CAP, dtype=jnp.int32)[None, None, :]
    owner = (source + offsets[round_index]) % N_WIDE
    local_index = round_index * CAP + within
    owner_full = jnp.broadcast_to(owner, (N_WIDE, rounds, CAP))
    local_full = jnp.broadcast_to(local_index, (N_WIDE, rounds, CAP))
    source_full = jnp.broadcast_to(source, (N_WIDE, rounds, CAP))
    slot_value = slot_orders[owner_full, local_full]
    place_value = places[source_full, local_full]
    target = owner_full * COLS_DEV + slot_value
    where_to = source_full * COLS_DEV + place_value
    return jnp.zeros((N_WIDE * COLS_DEV,), jnp.int32).at[where_to.reshape(-1)].set(target.reshape(-1))


def with_ends(values, own_key, smallest, largest):
    longest = values.shape.index(max(values.shape))
    spots = []
    for shift in (0, 1):
        where = [jax.random.randint(jax.random.fold_in(own_key, axis), (), 0, length) for axis, length in enumerate(values.shape)]
        where[longest] = (where[longest] + shift) % values.shape[longest]
        spots.append(tuple(where))
    return values.at[spots[0]].set(smallest).at[spots[1]].set(largest)


def block_levels(rng, dims, cuts, least, high):
    gain = 1.0
    for position, blocks in cuts:
        heights = jax.random.uniform(jax.random.fold_in(jax.random.fold_in(rng, 6), position), (blocks,), jnp.float32, least / len(cuts), high / len(cuts))
        gain = gain * jnp.repeat(jnp.exp(heights), dims[position] // blocks).reshape((-1,) + (1,) * (len(dims) - 1 - position))
    return gain


def bell_draw(own_key, extent, deviation, limit, cuts=(), held_as=jnp.bfloat16):
    values = deviation * jax.random.normal(own_key, extent, jnp.float32)
    if cuts:
        values = values * block_levels(own_key, extent, cuts, -0.22, 0.18)
    return jnp.clip(values, -limit, limit).astype(held_as)


def setup_inputs(seed: int = 0) -> dict:
    key_list = jax.random.split(jax.random.key(seed), 8)
    return {
        "gcm_state": bell_draw(key_list[0], (NCOL, 2 * LEV), 1.0, 6.0, ((0, 8),), jnp.float32),
        "crm_state": bell_draw(key_list[1], (2, CLEV, CX, NCOL), 1.0, 6.0, ((2, 4), (3, 8))),
        "courant": jnp.clip(0.1 + 0.5 * jax.random.uniform(key_list[2], (CLEV, NCOL), jnp.float32) ** block_levels(key_list[2], (CLEV, NCOL), ((1, 8),), -0.2, 0.2), 0.1, 0.6),
        "cloud_mask": with_ends((jax.random.randint(key_list[3], (CLEV, NCOL), 0, 2) < 1).astype(jnp.int32), jax.random.fold_in(key_list[3], 1), 0, 1),
        "level_down": bell_draw(key_list[4], (CLEV, LEV), LEV ** -0.5, 0.75, (), jnp.float32),
        "level_up": bell_draw(key_list[5], (LEV, CLEV), CLEV ** -0.5, 0.75, (), jnp.float32),
        "column_map": draw_column_map(jax.random.fold_in(key_list[7], 71), 0),
    }


def horizontal(padded, courant_now):
    left_cells = padded[:, :, :-2]
    middle = padded[:, :, 1:-1]
    right_cells = padded[:, :, 2:]
    return middle + courant_now[None, :, None, :] * (left_cells - middle) + 0.15 * (right_cells - 2.0 * middle + left_cells)


def column_physics(fields, forcing, cloudy):
    above_cells = jnp.concatenate([fields[:, 1:], fields[:, -1:]], axis=1)
    below_cells = jnp.concatenate([fields[:, :1], fields[:, :-1]], axis=1)
    fields = fields + 0.1 * (above_cells - 2.0 * fields + below_cells)
    fields = fields + 0.25 * forcing[:, :, None, :]
    moisture = fields[1]
    condensed = cloudy[:, None, :] * 0.3 * jnp.maximum(moisture, 0.0)
    return jnp.stack([fields[0] + 2.0 * condensed, moisture - condensed])


def crm_block(blocks):
    start_fields, forcing, courant_now, cloudy = blocks
    initial = start_fields.astype(jnp.float32)
    fields = initial
    for substep in range(SUB):
        padded = jnp.concatenate([fields[:, :, -1:], fields, fields[:, :, :1]], axis=2)
        fields = column_physics(horizontal(padded, courant_now), forcing, cloudy)
    return fields.astype(jnp.bfloat16), jnp.sum(fields - initial, axis=2)


def reference(gcm_state, crm_state, courant, cloud_mask, level_down, level_up, column_map):
    column_count = gcm_state.shape[0]
    sent_rows = lax.optimization_barrier(gcm_state.astype(jnp.bfloat16)).astype(jnp.float32)
    inverse = jnp.zeros((column_count,), jnp.int32).at[column_map].set(jnp.arange(column_count, dtype=jnp.int32))
    slot_rows = sent_rows[inverse].reshape(column_count, 2, LEV)
    forcing = jnp.einsum("sfm,lm->fls", slot_rows, level_down, precision=lax.Precision.HIGHEST)
    blocks_count = column_count // COLS_DEV

    def split_slots(values):
        return jnp.moveaxis(values.reshape(values.shape[:-1] + (blocks_count, COLS_DEV)), -2, 0)

    new_blocks, diff_blocks = lax.map(crm_block, (split_slots(crm_state), split_slots(forcing), split_slots(courant), split_slots(cloud_mask.astype(jnp.float32))))
    crm_new = jnp.moveaxis(new_blocks, 0, -2).reshape(crm_state.shape)
    diff_sums = jnp.moveaxis(diff_blocks, 0, -2).reshape(2, CLEV, column_count)
    tendency = jnp.einsum("fls,ml->sfm", diff_sums, level_up, precision=lax.Precision.HIGHEST) * (1.0 / (CX * SUB))
    gcm_tendency = tendency.reshape(column_count, 2 * LEV)[column_map].astype(jnp.bfloat16)
    return gcm_tendency, crm_new
```

```python
import functools

import jax
import jax.numpy as jnp
from jax import lax
from jax.experimental import pallas as pl
from jax.experimental.pallas import tpu as pltpu
from jax.sharding import PartitionSpec as P

SUB = 4
MESH = pl.DeviceIdType.MESH
EXACT = lax.Precision.HIGHEST
SCALE = 0.015


def on_rows(ref, start, size):
    return ref.at[pl.ds(pl.multiple_of(start, size), size)]


def greet(axes):
    barrier = pltpu.get_barrier_semaphore()
    count = 0
    for axis, steps in axes:
        size = lax.axis_size(axis)
        me = lax.axis_index(axis)
        for step in steps:
            pl.semaphore_signal(
                barrier, inc=1, device_id={axis: lax.rem(me + step, size)}, device_id_type=MESH
            )
            count += 1
    pl.semaphore_wait(barrier, count)


def peers(axis, source, place, send_sem, recv_sem):
    size = lax.axis_size(axis)
    me = lax.axis_index(axis)
    out, arriving = [], []
    for step in range(1, size):
        target = lax.rem(me + step, size)
        origin = lax.rem(me + size - step, size)
        out.append(
            pltpu.make_async_remote_copy(
                src_ref=source(target),
                dst_ref=place(me),
                send_sem=send_sem.at[step],
                recv_sem=recv_sem.at[me],
                device_id={axis: target},
                device_id_type=MESH,
            )
        )
        arriving.append(
            pltpu.make_async_remote_copy(
                src_ref=source(target),
                dst_ref=place(origin),
                send_sem=send_sem.at[step],
                recv_sem=recv_sem.at[origin],
                device_id={axis: target},
                device_id_type=MESH,
            )
        )
    return out, arriving


def send_kernel(
    slots_ref, gcm_ref, down_ref, crm_ref,
    low_ref, high_ref, forcing_ref, place_ref, pick_ref,
    top, bottom, top_out, bottom_out, packed, landed, ranks,
    local_sem, send_sem, recv_sem, halo_send, halo_recv,
):
    wide = lax.axis_size("wide")
    narrow = lax.axis_size("narrow")
    me = lax.axis_index("wide")
    depth = lax.axis_index("narrow")
    columns = gcm_ref.shape[0]
    rows = packed.shape[0] // wide
    levels, cells = crm_ref.shape[1], crm_ref.shape[2]
    top_copy = pltpu.make_async_copy(crm_ref.at[:, :, 0:16, :], top, local_sem.at[0])
    bottom_copy = pltpu.make_async_copy(
        crm_ref.at[:, :, cells - 16 : cells, :], bottom, local_sem.at[1]
    )
    top_copy.start()
    bottom_copy.start()
    greet((("wide", range(1, wide)), ("narrow", (1, narrow - 1))))

    mine = slots_ref[pl.ds(me, 1), :]
    owner_first = lax.broadcasted_iota(jnp.int32, (wide, columns), 0) * columns
    goes = (mine >= owner_first) & (mine < owner_first + columns)
    before = (
        lax.broadcasted_iota(jnp.int32, (columns, columns), 0)
        < lax.broadcasted_iota(jnp.int32, (columns, columns), 1)
    ).astype(jnp.float32).astype(jnp.bfloat16)

    def ranked(member):
        member = member.astype(jnp.float32)
        order = jnp.dot(member.astype(jnp.bfloat16), before, preferred_element_type=jnp.float32)
        return jnp.where(member > 0.0, order, -1.0)

    within = lax.broadcasted_iota(jnp.int32, (rows, columns), 0).astype(jnp.float32)
    ranks[...] = ranked(goes)
    for target in range(wide):
        hit = (ranks[target : target + 1, :] == within).astype(jnp.float32).astype(jnp.bfloat16)
        pick_ref[target * rows : (target + 1) * rows, :] = hit
    sent = gcm_ref[...].astype(jnp.bfloat16)
    packed[...] = jnp.dot(pick_ref[...], sent, preferred_element_type=jnp.float32).astype(
        jnp.bfloat16
    )
    states, states_in = peers(
        "wide",
        lambda target: on_rows(packed, target * rows, rows),
        lambda origin: on_rows(landed, origin * rows, rows),
        send_sem,
        recv_sem,
    )
    for copy in states:
        copy.start()
    own_rows = pl.ds(pl.multiple_of(me * rows, rows), rows)
    landed[own_rows, :] = packed[own_rows, :]

    first_half = lax.broadcasted_iota(jnp.int32, (8, columns), 0) < 4
    top_copy.wait()
    bottom_copy.wait()
    for field in range(2):

        def gather(group, carry):
            low_parts, high_parts = [], []
            for pair in range(2):
                level = group * 4 + pair * 2
                a = top[field, level].astype(jnp.float32)[0:8]
                b = top[field, level + 1].astype(jnp.float32)[0:8]
                low_parts.append(jnp.where(first_half, a, pltpu.roll(b, 4, 0)))
                a = bottom[field, level].astype(jnp.float32)[8:16]
                b = bottom[field, level + 1].astype(jnp.float32)[8:16]
                high_parts.append(jnp.where(first_half, pltpu.roll(a, 4, 0), b))
            at = pl.ds(pl.multiple_of(field * levels * 4 + group * 16, 16), 16)
            top_out[at, :] = jnp.concatenate(low_parts, axis=0).astype(jnp.bfloat16)
            bottom_out[at, :] = jnp.concatenate(high_parts, axis=0).astype(jnp.bfloat16)
            return carry

        lax.fori_loop(0, levels // 4, gather, 0)

    def halo(source, dest, which, step):
        return pltpu.make_async_remote_copy(
            src_ref=source,
            dst_ref=dest,
            send_sem=halo_send.at[which],
            recv_sem=halo_recv.at[which],
            device_id={"narrow": lax.rem(depth + step, narrow)},
            device_id_type=MESH,
        )

    onward = halo(bottom_out, low_ref, 0, 1)
    backward = halo(top_out, high_ref, 1, narrow - 1)
    onward.start()
    backward.start()

    first = me * columns
    slots = slots_ref[...]
    ranks[...] = ranked((slots >= first) & (slots < first + columns))
    slot_number = lax.broadcasted_iota(jnp.int32, (columns, columns), 0) + first
    for origin in range(wide):
        hit = (ranks[origin : origin + 1, :] == within).astype(jnp.float32).astype(jnp.bfloat16)
        spot = (slots_ref[origin : origin + 1, :] == slot_number).astype(jnp.float32)
        place_ref[origin * rows : (origin + 1) * rows, :] = lax.dot_general(
            hit,
            spot.astype(jnp.bfloat16),
            (((1,), (1,)), ((), ())),
            preferred_element_type=jnp.float32,
        ).astype(jnp.bfloat16)
    for copy in states_in:
        copy.wait_recv()
    by_slot = lax.dot_general(
        landed[...],
        place_ref[...],
        (((0,), (0,)), ((), ())),
        preferred_element_type=jnp.float32,
    )
    span = by_slot.shape[0] // 2
    for field in range(2):
        forcing_ref[field] = jnp.dot(
            down_ref[...],
            by_slot[field * span : (field + 1) * span],
            precision=EXACT,
            preferred_element_type=jnp.float32,
        )
    for copy in states:
        copy.wait_send()
    onward.wait()
    backward.wait()


def physics_kernel(
    crm_ref, low_ref, high_ref, forcing_ref, courant_ref, cloud_ref,
    out_ref, change_ref,
    slab, state, left_gain, middle_gain, keep, push,
):
    levels, cells = crm_ref.shape[1], crm_ref.shape[2]
    parts = (cells + 2 * SUB) // 8
    courant = courant_ref[...]
    left_gain[...] = (courant + 0.15) * (1.0 / 0.15)
    middle_gain[...] = (0.7 - courant) * (1.0 / 0.15)
    keep[...] = 1.0 - 0.3 * cloud_ref[...].astype(jnp.float32)
    for substep in range(SUB):
        gain = 0.25 / SCALE ** (substep + 1)
        push[2 * substep + 1] = gain * forcing_ref[1]
        push[2 * substep] = gain * (forcing_ref[0] + 2.0 * forcing_ref[1])

    for field in range(2):

        def spread(group, carry):
            at = pl.ds(pl.multiple_of(field * levels * 4 + group * 16, 16), 16)
            low = low_ref[at, :].astype(jnp.float32)
            high = high_ref[at, :].astype(jnp.float32)
            for step in range(4):
                level = group * 4 + step
                from_row = 8 * (step // 2)
                low_part = low[from_row : from_row + 8]
                high_part = high[from_row : from_row + 8]
                if step % 2 == 0:
                    low_part = pltpu.roll(low_part, 4, 0)
                else:
                    high_part = pltpu.roll(high_part, 4, 0)
                slab[field * levels + level, 0:8, :] = low_part
                slab[field * levels + level, cells + 8 : cells + 16, :] = high_part
                slab[field * levels + level, 8 : cells + 8, :] = crm_ref[field, level].astype(
                    jnp.float32
                )
            return carry

        lax.fori_loop(0, levels // 4, spread, 0)

    def strided(field, level, part):
        return slab[field * levels + level, pl.ds(4 + part, 8, stride=parts), :]

    for substep in range(SUB):
        for field in (1, 0):

            def fetch(level):
                if substep > 0:
                    return [state[field * levels + level, part] for part in range(parts)]
                moist = [strided(1, level, part) for part in range(parts)]
                if field == 1:
                    return moist
                return [strided(0, level, part) + 2.0 * moist[part] for part in range(parts)]

            def across(level):
                cell = fetch(level)
                gain_left = left_gain[pl.ds(level, 1), :]
                gain_middle = middle_gain[pl.ds(level, 1), :]
                before = [pltpu.roll(cell[-1], 1, 0)] + cell[:-1]
                after = cell[1:] + [pltpu.roll(cell[0], 7, 0)]
                return [
                    after[part] + gain_left * before[part] + gain_middle * cell[part]
                    for part in range(parts)
                ]

            def finish(level, below, here, above):
                forced = push[2 * substep + field, pl.ds(level, 1), :]
                kept = keep[pl.ds(level, 1), :]
                for part in range(parts):
                    value = (below[part] + above[part]) + (8.0 * here[part] + forced)
                    if field == 1:
                        value = jnp.minimum(value, kept * value)
                    if substep == SUB - 1:
                        value = value * (SCALE**SUB)
                        if field == 1:
                            state[levels + level, part] = value
                        else:
                            value = value - 2.0 * state[levels + level, part]
                        slab[
                            field * levels + level, pl.ds(4 + part, 8, stride=parts), :
                        ] = value
                    else:
                        state[field * levels + level, part] = value

            def climb(level, carry):
                below, here = carry
                above = across(level + 1)
                finish(level, below, here, above)
                return here, above

            first = across(0)
            second = across(1)
            finish(0, first, first, second)
            below, here = lax.fori_loop(1, levels - 1, climb, (first, second), unroll=2)
            finish(levels - 1, below, here, here)

    for field in range(2):

        def close(level, carry):
            final = slab[field * levels + level, 8 : cells + 8, :]
            out_ref[field, level] = final.astype(jnp.bfloat16)
            moved = final - crm_ref[field, level].astype(jnp.float32)
            change_ref[field, pl.ds(level, 1), :] = jnp.sum(moved, axis=0, keepdims=True)
            return carry

        lax.fori_loop(0, levels, close, 0, unroll=2)


def return_kernel(
    share, change_ref, up_ref, place_ref, pick_ref,
    out_ref,
    sums, packed, landed,
    sum_send, sum_recv, send_sem, recv_sem,
):
    wide = lax.axis_size("wide")
    narrow = lax.axis_size("narrow")
    me = lax.axis_index("wide")
    depth = lax.axis_index("narrow")
    rows = packed.shape[0] // wide
    greet((("wide", range(1, wide)), ("narrow", range(1, narrow))))
    partial, partial_in = peers(
        "narrow", lambda target: change_ref, lambda origin: sums.at[origin], sum_send, sum_recv
    )
    for copy in partial:
        copy.start()
    sums[depth] = change_ref[...]
    for copy in partial_in:
        copy.wait_recv()
    total = sums[0]
    for origin in range(1, narrow):
        total = total + sums[origin]
    tendency = jnp.concatenate(
        [
            jnp.dot(
                up_ref[...], total[field], precision=EXACT, preferred_element_type=jnp.float32
            )
            for field in range(2)
        ],
        axis=0,
    )
    tendency = (tendency * share).astype(jnp.bfloat16)
    packed[...] = lax.dot_general(
        place_ref[...], tendency, (((1,), (1,)), ((), ())), preferred_element_type=jnp.float32
    ).astype(jnp.bfloat16)
    back, back_in = peers(
        "wide",
        lambda target: on_rows(packed, target * rows, rows),
        lambda origin: on_rows(landed, origin * rows, rows),
        send_sem,
        recv_sem,
    )
    for copy in back:
        copy.start()
    own_rows = pl.ds(pl.multiple_of(me * rows, rows), rows)
    landed[own_rows, :] = packed[own_rows, :]
    for copy in back_in:
        copy.wait_recv()
    out_ref[...] = lax.dot_general(
        pick_ref[...], landed[...], (((0,), (0,)), ((), ())), preferred_element_type=jnp.float32
    ).astype(jnp.bfloat16)
    for copy in partial + back:
        copy.wait_send()


def shards(gcm_state, crm_state, courant, cloud_mask, level_down, level_up, column_map):
    wide = lax.axis_size("wide")
    narrow = lax.axis_size("narrow")
    columns, width = gcm_state.shape
    _, levels, cells, _ = crm_state.shape
    capacity = -(-2 * columns // wide)
    rows = -(-capacity // 16) * 16
    total = wide * rows
    halo = 2 * levels * SUB
    vmem = pl.BlockSpec(memory_space=pltpu.VMEM)
    struct = jax.ShapeDtypeStruct
    dma = pltpu.SemaphoreType.DMA
    low, high, forcing, place, pick = pl.pallas_call(
        send_kernel,
        out_shape=(
            struct((halo, columns), jnp.bfloat16),
            struct((halo, columns), jnp.bfloat16),
            struct((2, levels, columns), jnp.float32),
            struct((total, columns), jnp.bfloat16),
            struct((total, columns), jnp.bfloat16),
        ),
        in_specs=[vmem, vmem, vmem, pl.BlockSpec(memory_space=pl.ANY)],
        out_specs=(vmem,) * 5,
        scratch_shapes=[
            pltpu.VMEM((2, levels, 16, columns), jnp.bfloat16),
            pltpu.VMEM((2, levels, 16, columns), jnp.bfloat16),
            pltpu.VMEM((halo, columns), jnp.bfloat16),
            pltpu.VMEM((halo, columns), jnp.bfloat16),
            pltpu.VMEM((total, width), jnp.bfloat16),
            pltpu.VMEM((total, width), jnp.bfloat16),
            pltpu.VMEM((wide, columns), jnp.float32),
            dma((2,)),
            dma((wide,)),
            dma((wide,)),
            dma((2,)),
            dma((2,)),
        ],
        compiler_params=pltpu.CompilerParams(
            collective_id=0, has_side_effects=True, vmem_limit_bytes=24 * 2**20
        ),
        name="send",
    )(column_map.reshape(wide, columns), gcm_state, level_down, crm_state)
    crm_new, change = pl.pallas_call(
        physics_kernel,
        out_shape=(
            struct(crm_state.shape, jnp.bfloat16),
            struct((2, levels, columns), jnp.float32),
        ),
        in_specs=[vmem] * 6,
        out_specs=(vmem,) * 2,
        scratch_shapes=[
            pltpu.VMEM((2 * levels, cells + 16, columns), jnp.float32),
            pltpu.VMEM((2 * levels, (cells + 2 * SUB) // 8, 8, columns), jnp.float32),
            pltpu.VMEM((levels, columns), jnp.float32),
            pltpu.VMEM((levels, columns), jnp.float32),
            pltpu.VMEM((levels, columns), jnp.float32),
            pltpu.VMEM((2 * SUB, levels, columns), jnp.float32),
        ],
        compiler_params=pltpu.CompilerParams(vmem_limit_bytes=32 * 2**20),
        name="physics",
    )(crm_state, low, high, forcing, courant, cloud_mask)
    gcm_tendency = pl.pallas_call(
        functools.partial(return_kernel, 1.0 / (cells * narrow * SUB)),
        out_shape=struct((columns, width), jnp.bfloat16),
        in_specs=[vmem] * 4,
        out_specs=vmem,
        scratch_shapes=[
            pltpu.VMEM((narrow, 2, levels, columns), jnp.float32),
            pltpu.VMEM((total, width), jnp.bfloat16),
            pltpu.VMEM((total, width), jnp.bfloat16),
            dma((narrow,)),
            dma((narrow,)),
            dma((wide,)),
            dma((wide,)),
        ],
        compiler_params=pltpu.CompilerParams(
            collective_id=1, has_side_effects=True, vmem_limit_bytes=24 * 2**20
        ),
        name="back",
    )(change, level_up, place, pick)
    return gcm_tendency, crm_new


def solution(mesh):
    placed = (
        P("wide", None),
        P(None, None, "narrow", "wide"),
        P(None, "wide"),
        P(None, "wide"),
        P(),
        P(),
        P(),
    )
    return jax.shard_map(
        shards,
        mesh=mesh,
        in_specs=placed,
        out_specs=(P("wide", None), P(None, None, "narrow", "wide")),
        check_vma=False,
    )
```

```python
import jax
import jax.numpy as jnp
from jax import lax
from jax.experimental import pallas as pl
from jax.experimental.pallas import tpu as pltpu
from jax.sharding import PartitionSpec as P

SUB = 4
MESH = pl.DeviceIdType.MESH
EXACT = lax.Precision.HIGHEST
SCALE = 0.015


def on_rows(ref, start, size):
    return ref.at[pl.ds(pl.multiple_of(start, size), size)]


def peers(axis, source, place, send_sem, recv_sem):
    size = lax.axis_size(axis)
    me = lax.axis_index(axis)
    out, arriving = [], []
    for step in range(1, size):
        target = lax.rem(me + step, size)
        origin = lax.rem(me + size - step, size)
        out.append(
            pltpu.make_async_remote_copy(
                src_ref=source(target),
                dst_ref=place(me),
                send_sem=send_sem.at[step],
                recv_sem=recv_sem.at[me],
                device_id={axis: target},
                device_id_type=MESH,
            )
        )
        arriving.append(
            pltpu.make_async_remote_copy(
                src_ref=source(target),
                dst_ref=place(origin),
                send_sem=send_sem.at[step],
                recv_sem=recv_sem.at[origin],
                device_id={axis: target},
                device_id_type=MESH,
            )
        )
    return out, arriving


def signal_peers():
    barrier = pltpu.get_barrier_semaphore()
    for axis in ("wide", "narrow"):
        size = lax.axis_size(axis)
        me = lax.axis_index(axis)
        for step in range(1, size):
            pl.semaphore_signal(
                barrier, inc=1, device_id={axis: lax.rem(me + step, size)}, device_id_type=MESH
            )


def step_kernel(
    slots_hbm, gcm_hbm, down_hbm, up_hbm, courant_hbm, cloud_hbm, crm_hbm,
    tendency_ref, out_ref,
    slots_ref, gcm_ref, down_ref, up_ref, courant_ref, cloud_ref, crm_ref,
    low_out, high_out, low_in, high_in,
    pick, place, packed, landed, packed_back, landed_back, ranks,
    slab, state, left_gain, middle_gain, keep, push, source_term,
    start_sum, start_sums, moist_sum, moist_sums,
    local_sem, send_sem, recv_sem, back_send, back_recv,
    halo_send, halo_recv, start_send, start_recv, moist_send, moist_recv,
):
    wide = lax.axis_size("wide")
    narrow = lax.axis_size("narrow")
    me = lax.axis_index("wide")
    depth = lax.axis_index("narrow")
    columns = gcm_ref.shape[1]
    rows = packed.shape[0] // wide
    levels, cells = crm_ref.shape[1], crm_ref.shape[2]
    parts = (cells + 2 * SUB) // 8
    bf16 = jnp.bfloat16

    pairs = (
        (crm_hbm.at[1], crm_ref.at[1]),
        (slots_hbm, slots_ref),
        (gcm_hbm, gcm_ref),
        (crm_hbm.at[0], crm_ref.at[0]),
        (courant_hbm, courant_ref),
        (cloud_hbm, cloud_ref),
        (down_hbm, down_ref),
        (up_hbm, up_ref),
    )
    inward = [
        pltpu.make_async_copy(source, dest, local_sem.at[index])
        for index, (source, dest) in enumerate(pairs)
    ]
    crm_moist, slots_copy, gcm_copy, crm_warm, courant_copy, cloud_copy, down_copy, up_copy = inward
    for copy in inward:
        copy.start()
    signal_peers()

    first_half = lax.broadcasted_iota(jnp.int32, (8, columns), 0) < 4

    def pack_halo(field):
        def gather(group, carry):
            low_parts, high_parts = [], []
            for pair in range(2):
                level = group * 4 + pair * 2
                a = crm_ref[field, level, 0:16, :].astype(jnp.float32)[0:8]
                b = crm_ref[field, level + 1, 0:16, :].astype(jnp.float32)[0:8]
                low_parts.append(jnp.where(first_half, a, pltpu.roll(b, 4, 0)))
                a = crm_ref[field, level, cells - 16 : cells, :].astype(jnp.float32)[8:16]
                b = crm_ref[field, level + 1, cells - 16 : cells, :].astype(jnp.float32)[8:16]
                high_parts.append(jnp.where(first_half, pltpu.roll(a, 4, 0), b))
            at = pl.ds(pl.multiple_of(group * 16, 16), 16)
            low_out[field, at, :] = jnp.concatenate(low_parts, axis=0).astype(bf16)
            high_out[field, at, :] = jnp.concatenate(high_parts, axis=0).astype(bf16)
            return carry

        lax.fori_loop(0, levels // 4, gather, 0)

    def halo_copies(field):
        def halo(source, dest, which, step):
            return pltpu.make_async_remote_copy(
                src_ref=source.at[field],
                dst_ref=dest.at[field],
                send_sem=halo_send.at[which],
                recv_sem=halo_recv.at[which],
                device_id={"narrow": lax.rem(depth + step, narrow)},
                device_id_type=MESH,
            )

        return (
            halo(high_out, low_in, 2 * field, 1),
            halo(low_out, high_in, 2 * field + 1, narrow - 1),
        )

    crm_moist.wait()
    pack_halo(1)
    pl.semaphore_wait(pltpu.get_barrier_semaphore(), wide + narrow - 2)
    moist_halo = halo_copies(1)
    for copy in moist_halo:
        copy.start()

    slots_copy.wait()
    mine = slots_ref[pl.ds(me, 1), :]
    owner_first = lax.broadcasted_iota(jnp.int32, (wide, columns), 0) * columns
    goes = (mine >= owner_first) & (mine < owner_first + columns)
    before = (
        lax.broadcasted_iota(jnp.int32, (columns, columns), 0)
        < lax.broadcasted_iota(jnp.int32, (columns, columns), 1)
    ).astype(jnp.float32).astype(bf16)

    def ranked(member):
        member = member.astype(jnp.float32)
        order = jnp.dot(member.astype(bf16), before, preferred_element_type=jnp.float32)
        return jnp.where(member > 0.0, order, -1.0)

    within = lax.broadcasted_iota(jnp.int32, (rows, columns), 0).astype(jnp.float32)
    ranks[...] = ranked(goes)
    for target in range(wide):
        hit = (ranks[target : target + 1, :] == within).astype(jnp.float32).astype(bf16)
        pick[target * rows : (target + 1) * rows, :] = hit
    gcm_copy.wait()
    packed[...] = lax.dot_general(
        pick[...],
        gcm_ref[...].astype(bf16),
        (((1,), (1,)), ((), ())),
        preferred_element_type=jnp.float32,
    ).astype(bf16)
    states, states_in = peers(
        "wide",
        lambda target: on_rows(packed, target * rows, rows),
        lambda origin: on_rows(landed, origin * rows, rows),
        send_sem,
        recv_sem,
    )
    for copy in states:
        copy.start()
    own_rows = pl.ds(pl.multiple_of(me * rows, rows), rows)
    landed[own_rows, :] = packed[own_rows, :]

    crm_warm.wait()
    pack_halo(0)
    warm_halo = halo_copies(0)
    for copy in warm_halo:
        copy.start()

    def spread(level, carry):
        warm = crm_ref[0, level].astype(jnp.float32)
        moist = crm_ref[1, level].astype(jnp.float32)
        slab[level, 8 : cells + 8, :] = warm
        slab[levels + level, 8 : cells + 8, :] = moist
        start_sum[pl.ds(level, 1), :] = jnp.sum(warm + 2.0 * moist, axis=0, keepdims=True)
        return carry

    lax.fori_loop(0, levels, spread, 0, unroll=2)
    starts, starts_in = peers(
        "narrow", lambda target: start_sum, lambda origin: start_sums.at[origin],
        start_send, start_recv,
    )
    for copy in starts:
        copy.start()
    start_sums[depth] = start_sum[...]

    courant_copy.wait()
    cloud_copy.wait()
    courant = courant_ref[...]
    left_gain[...] = (courant + 0.15) * (1.0 / 0.15)
    middle_gain[...] = (0.7 - courant) * (1.0 / 0.15)
    keep[...] = 1.0 - 0.3 * cloud_ref[...].astype(jnp.float32)

    first = me * columns
    slots = slots_ref[...]
    ranks[...] = ranked((slots >= first) & (slots < first + columns))
    slot_number = lax.broadcasted_iota(jnp.int32, (columns, columns), 0) + first
    for origin in range(wide):
        hit = (ranks[origin : origin + 1, :] == within).astype(jnp.float32).astype(bf16)
        spot = (slots_ref[origin : origin + 1, :] == slot_number).astype(jnp.float32)
        place[origin * rows : (origin + 1) * rows, :] = lax.dot_general(
            hit,
            spot.astype(bf16),
            (((1,), (1,)), ((), ())),
            preferred_element_type=jnp.float32,
        ).astype(bf16)
    down_copy.wait()
    for copy in states_in:
        copy.wait_recv()
    by_slot = lax.dot_general(
        landed[...], place[...], (((0,), (0,)), ((), ())), preferred_element_type=jnp.float32
    )
    span = by_slot.shape[0] // 2
    warm_force, moist_force = [
        jnp.dot(
            down_ref[...],
            by_slot[field * span : (field + 1) * span],
            precision=EXACT,
            preferred_element_type=jnp.float32,
        )
        for field in range(2)
    ]
    sum_force = warm_force + 2.0 * moist_force
    source_term[...] = (0.25 * cells * narrow) * sum_force
    for substep in range(SUB):
        gain = 0.25 / SCALE ** (substep + 1)
        push[2 * substep + 1] = gain * moist_force
        push[2 * substep] = gain * sum_force

    def surround(field):
        def insert(group, carry):
            at = pl.ds(pl.multiple_of(group * 16, 16), 16)
            low = low_in[field, at, :].astype(jnp.float32)
            high = high_in[field, at, :].astype(jnp.float32)
            for step in range(4):
                level = group * 4 + step
                from_row = 8 * (step // 2)
                low_part = low[from_row : from_row + 8]
                high_part = high[from_row : from_row + 8]
                if step % 2 == 0:
                    low_part = pltpu.roll(low_part, 4, 0)
                else:
                    high_part = pltpu.roll(high_part, 4, 0)
                slab[field * levels + level, 0:8, :] = low_part
                slab[field * levels + level, cells + 8 : cells + 16, :] = high_part
            return carry

        lax.fori_loop(0, levels // 4, insert, 0)

    def strided(field, level, part):
        return slab[field * levels + level, pl.ds(4 + part, 8, stride=parts), :]

    def advance(field, substep):
        last = substep == SUB - 1

        def fetch(level):
            if substep > 0:
                return [state[field * levels + level, part] for part in range(parts)]
            cell = [strided(field, level, part) for part in range(parts)]
            if field == 1:
                return cell
            return [cell[part] + 2.0 * keep_moist(level, part) for part in range(parts)]

        def across(level):
            cell = fetch(level)
            gain_left = left_gain[pl.ds(level, 1), :]
            gain_middle = middle_gain[pl.ds(level, 1), :]
            behind = [pltpu.roll(cell[-1], 1, 0)] + cell[:-1]
            ahead = cell[1:] + [pltpu.roll(cell[0], 7, 0)]
            return [
                ahead[part] + gain_left * behind[part] + gain_middle * cell[part]
                for part in range(parts)
            ]

        def finish(level, below, here, above):
            forced = push[2 * substep + field, pl.ds(level, 1), :]
            kept = keep[pl.ds(level, 1), :]
            for part in range(parts):
                value = (below[part] + above[part]) + (8.0 * here[part] + forced)
                if field == 1:
                    value = jnp.minimum(value, kept * value)
                if not last:
                    state[field * levels + level, part] = value
                    continue
                value = value * (SCALE**SUB)
                if field == 1:
                    state[levels + level, part] = value
                    slab[2 * levels + level, pl.ds(4 + part, 8, stride=parts), :] = value
                else:
                    value = value - 2.0 * state[levels + level, part]
                    slab[level, pl.ds(4 + part, 8, stride=parts), :] = value

        def climb(level, carry):
            below, here = carry
            above = across(level + 1)
            finish(level, below, here, above)
            return here, above

        bottom = across(0)
        second = across(1)
        finish(0, bottom, bottom, second)
        below, here = lax.fori_loop(1, levels - 1, climb, (bottom, second), unroll=2)
        finish(levels - 1, below, here, here)

    def keep_moist(level, part):
        return strided(1, level, part)

    for copy in moist_halo:
        copy.wait_recv()
    surround(1)
    for substep in range(SUB):
        advance(1, substep)

    def close_moist(level, carry):
        final = slab[2 * levels + level, 8 : cells + 8, :]
        out_ref[1, level] = final.astype(bf16)
        moved = final - slab[levels + level, 8 : cells + 8, :]
        moist_sum[pl.ds(level, 1), :] = jnp.sum(moved, axis=0, keepdims=True)
        return carry

    lax.fori_loop(0, levels, close_moist, 0, unroll=2)
    moists, moists_in = peers(
        "narrow", lambda target: moist_sum, lambda origin: moist_sums.at[origin],
        moist_send, moist_recv,
    )
    for copy in moists:
        copy.start()
    moist_sums[depth] = moist_sum[...]

    for copy in warm_halo:
        copy.wait_recv()
    surround(0)
    for substep in range(SUB - 1):
        advance(0, substep)

    for copy in starts_in + moists_in:
        copy.wait_recv()
    total, moist_change = start_sums[0], moist_sums[0]
    for origin in range(1, narrow):
        total = total + start_sums[origin]
        moist_change = moist_change + moist_sums[origin]
    sum_change = jnp.zeros_like(total)
    for substep in range(SUB):
        over = jnp.concatenate([total[1:], total[-1:]], axis=0)
        under = jnp.concatenate([total[:1], total[:-1]], axis=0)
        rise = 0.1 * (over - 2.0 * total + under) + source_term[...]
        total = total + rise
        sum_change = sum_change + rise
    up_copy.wait()
    changes = (sum_change - 2.0 * moist_change, moist_change)
    tendency = jnp.concatenate(
        [
            lax.dot_general(
                up_ref[...],
                change,
                (((0,), (0,)), ((), ())),
                precision=EXACT,
                preferred_element_type=jnp.float32,
            )
            for change in changes
        ],
        axis=0,
    )
    tendency = (tendency * (1.0 / (cells * narrow * SUB))).astype(bf16)
    packed_back[...] = lax.dot_general(
        place[...], tendency, (((1,), (1,)), ((), ())), preferred_element_type=jnp.float32
    ).astype(bf16)
    back, back_in = peers(
        "wide",
        lambda target: on_rows(packed_back, target * rows, rows),
        lambda origin: on_rows(landed_back, origin * rows, rows),
        back_send,
        back_recv,
    )
    for copy in back:
        copy.start()
    landed_back[own_rows, :] = packed_back[own_rows, :]

    advance(0, SUB - 1)

    def close_warm(level, carry):
        out_ref[0, level] = slab[level, 8 : cells + 8, :].astype(bf16)
        return carry

    lax.fori_loop(0, levels, close_warm, 0, unroll=2)
    for copy in back_in:
        copy.wait_recv()
    tendency_ref[...] = lax.dot_general(
        landed_back[...], pick[...], (((0,), (0,)), ((), ())), preferred_element_type=jnp.float32
    ).astype(bf16)
    for copy in [*moist_halo, *states, *warm_halo, *starts, *moists, *back]:
        copy.wait_send()


def shards(gcm_state, crm_state, courant, cloud_mask, level_down, level_up, column_map):
    wide = lax.axis_size("wide")
    narrow = lax.axis_size("narrow")
    columns, width = gcm_state.shape
    _, levels, cells, _ = crm_state.shape
    capacity = -(-2 * columns // wide)
    rows = -(-capacity // 16) * 16
    total = wide * rows
    operands = (
        column_map.reshape(wide, columns),
        gcm_state.T,
        level_down,
        level_up.T,
        courant,
        cloud_mask,
        crm_state,
    )
    vmem = pl.BlockSpec(memory_space=pltpu.VMEM)
    hbm = pl.BlockSpec(memory_space=pltpu.HBM)
    dma = pltpu.SemaphoreType.DMA
    parts = (cells + 2 * SUB) // 8

    def held(*shape, dtype=jnp.float32):
        return pltpu.VMEM(shape, dtype)

    halo = held(2, levels * SUB, columns, dtype=jnp.bfloat16)
    routed = held(total, columns, dtype=jnp.bfloat16)
    message = held(total, width, dtype=jnp.bfloat16)
    tendency, crm_new = pl.pallas_call(
        step_kernel,
        out_shape=(
            jax.ShapeDtypeStruct((width, columns), jnp.bfloat16),
            jax.ShapeDtypeStruct(crm_state.shape, jnp.bfloat16),
        ),
        in_specs=[hbm] * len(operands),
        out_specs=(vmem, vmem),
        scratch_shapes=[
            *(held(*operand.shape, dtype=operand.dtype) for operand in operands),
            *[halo] * 4,
            *[routed] * 2,
            *[message] * 4,
            held(wide, columns),
            held(3 * levels, cells + 16, columns),
            held(2 * levels, parts, 8, columns),
            *[held(levels, columns)] * 3,
            held(2 * SUB, levels, columns),
            held(levels, columns),
            held(levels, columns),
            held(narrow, levels, columns),
            held(levels, columns),
            held(narrow, levels, columns),
            dma((len(operands) + 1,)),
            *[dma((wide,))] * 4,
            *[dma((4,))] * 2,
            *[dma((narrow,))] * 4,
        ],
        compiler_params=pltpu.CompilerParams(
            collective_id=0, has_side_effects=True, vmem_limit_bytes=40 * 2**20
        ),
        name="step",
    )(*operands)
    return tendency.T, crm_new


def solution(mesh):
    placed = (
        P("wide", None),
        P(None, None, "narrow", "wide"),
        P(None, "wide"),
        P(None, "wide"),
        P(),
        P(),
        P(),
    )
    return jax.shard_map(
        shards,
        mesh=mesh,
        in_specs=placed,
        out_specs=(P("wide", None), P(None, None, "narrow", "wide")),
        check_vma=False,
    )
```

```python
import jax
import jax.numpy as jnp
from jax import lax
from jax.experimental import pallas as pl
from jax.experimental.pallas import tpu as pltpu
from jax.sharding import PartitionSpec as P

SUB = 4
MESH = pl.DeviceIdType.MESH
EXACT = lax.Precision.HIGHEST
SCALE = 0.015


def on_rows(ref, start, size):
    return ref.at[pl.ds(pl.multiple_of(start, size), size)]


def peers(axis, source, place, send_sem, recv_sem):
    size = lax.axis_size(axis)
    me = lax.axis_index(axis)
    out, arriving = [], []
    for step in range(1, size):
        target = lax.rem(me + step, size)
        origin = lax.rem(me + size - step, size)
        out.append(
            pltpu.make_async_remote_copy(
                src_ref=source(target),
                dst_ref=place(me),
                send_sem=send_sem.at[step],
                recv_sem=recv_sem.at[me],
                device_id={axis: target},
                device_id_type=MESH,
            )
        )
        arriving.append(
            pltpu.make_async_remote_copy(
                src_ref=source(target),
                dst_ref=place(origin),
                send_sem=send_sem.at[step],
                recv_sem=recv_sem.at[origin],
                device_id={axis: target},
                device_id_type=MESH,
            )
        )
    return out, arriving


def signal_peers():
    barrier = pltpu.get_barrier_semaphore()
    for axis in ("wide", "narrow"):
        size = lax.axis_size(axis)
        me = lax.axis_index(axis)
        for step in range(1, size):
            pl.semaphore_signal(
                barrier, inc=1, device_id={axis: lax.rem(me + step, size)}, device_id_type=MESH
            )


def step_kernel(
    slots_hbm, gcm_hbm, down_hbm, up_hbm, courant_hbm, cloud_hbm, crm_hbm,
    tendency_ref, out_hbm,
    out_ref, slots_ref, gcm_ref, down_ref, up_ref, courant_ref, cloud_ref, crm_ref,
    low_out, high_out, low_in, high_in,
    pick, place, packed, landed, packed_back, landed_back, ranks,
    slab, state, left_gain, middle_gain, keep, push, source_term,
    start_sum, start_sums, moist_sum, moist_sums,
    local_sem, send_sem, recv_sem, back_send, back_recv,
    halo_send, halo_recv, start_send, start_recv, moist_send, moist_recv,
):
    wide = lax.axis_size("wide")
    narrow = lax.axis_size("narrow")
    me = lax.axis_index("wide")
    depth = lax.axis_index("narrow")
    columns = gcm_ref.shape[1]
    rows = packed.shape[0] // wide
    levels, cells = crm_ref.shape[1], crm_ref.shape[2]
    parts = (cells + 2 * SUB) // 8
    bf16 = jnp.bfloat16

    pairs = (
        (crm_hbm.at[1], crm_ref.at[1]),
        (slots_hbm, slots_ref),
        (gcm_hbm, gcm_ref),
        (crm_hbm.at[0], crm_ref.at[0]),
        (courant_hbm, courant_ref),
        (cloud_hbm, cloud_ref),
        (down_hbm, down_ref),
        (up_hbm, up_ref),
    )
    inward = [
        pltpu.make_async_copy(source, dest, local_sem.at[index])
        for index, (source, dest) in enumerate(pairs)
    ]
    crm_moist, slots_copy, gcm_copy, crm_warm, courant_copy, cloud_copy, down_copy, up_copy = inward
    for copy in inward:
        copy.start()
    signal_peers()

    first_half = lax.broadcasted_iota(jnp.int32, (8, columns), 0) < 4

    def pack_halo(field):
        def gather(group, carry):
            low_parts, high_parts = [], []
            for pair in range(2):
                level = group * 4 + pair * 2
                a = crm_ref[field, level, 0:16, :].astype(jnp.float32)[0:8]
                b = crm_ref[field, level + 1, 0:16, :].astype(jnp.float32)[0:8]
                low_parts.append(jnp.where(first_half, a, pltpu.roll(b, 4, 0)))
                a = crm_ref[field, level, cells - 16 : cells, :].astype(jnp.float32)[8:16]
                b = crm_ref[field, level + 1, cells - 16 : cells, :].astype(jnp.float32)[8:16]
                high_parts.append(jnp.where(first_half, pltpu.roll(a, 4, 0), b))
            at = pl.ds(pl.multiple_of(group * 16, 16), 16)
            low_out[field, at, :] = jnp.concatenate(low_parts, axis=0).astype(bf16)
            high_out[field, at, :] = jnp.concatenate(high_parts, axis=0).astype(bf16)
            return carry

        lax.fori_loop(0, levels // 4, gather, 0)

    def halo_copies(field):
        def halo(source, dest, which, step):
            return pltpu.make_async_remote_copy(
                src_ref=source.at[field],
                dst_ref=dest.at[field],
                send_sem=halo_send.at[which],
                recv_sem=halo_recv.at[which],
                device_id={"narrow": lax.rem(depth + step, narrow)},
                device_id_type=MESH,
            )

        return (
            halo(high_out, low_in, 2 * field, 1),
            halo(low_out, high_in, 2 * field + 1, narrow - 1),
        )

    crm_moist.wait()
    pack_halo(1)
    pl.semaphore_wait(pltpu.get_barrier_semaphore(), wide + narrow - 2)
    moist_halo = halo_copies(1)
    for copy in moist_halo:
        copy.start()

    slots_copy.wait()
    mine = slots_ref[pl.ds(me, 1), :]
    owner_first = lax.broadcasted_iota(jnp.int32, (wide, columns), 0) * columns
    goes = (mine >= owner_first) & (mine < owner_first + columns)
    before = (
        lax.broadcasted_iota(jnp.int32, (columns, columns), 0)
        < lax.broadcasted_iota(jnp.int32, (columns, columns), 1)
    ).astype(jnp.float32).astype(bf16)

    def ranked(member):
        member = member.astype(jnp.float32)
        order = jnp.dot(member.astype(bf16), before, preferred_element_type=jnp.float32)
        return jnp.where(member > 0.0, order, -1.0)

    within = lax.broadcasted_iota(jnp.int32, (rows, columns), 0).astype(jnp.float32)
    ranks[...] = ranked(goes)
    for target in range(wide):
        hit = (ranks[target : target + 1, :] == within).astype(jnp.float32).astype(bf16)
        pick[target * rows : (target + 1) * rows, :] = hit
    gcm_copy.wait()
    packed[...] = lax.dot_general(
        pick[...],
        gcm_ref[...].astype(bf16),
        (((1,), (1,)), ((), ())),
        preferred_element_type=jnp.float32,
    ).astype(bf16)
    states, states_in = peers(
        "wide",
        lambda target: on_rows(packed, target * rows, rows),
        lambda origin: on_rows(landed, origin * rows, rows),
        send_sem,
        recv_sem,
    )
    for copy in states:
        copy.start()
    own_rows = pl.ds(pl.multiple_of(me * rows, rows), rows)
    landed[own_rows, :] = packed[own_rows, :]

    crm_warm.wait()
    pack_halo(0)
    warm_halo = halo_copies(0)
    for copy in warm_halo:
        copy.start()

    def spread(level, carry):
        warm = crm_ref[0, level].astype(jnp.float32)
        moist = crm_ref[1, level].astype(jnp.float32)
        slab[level, 8 : cells + 8, :] = warm
        slab[levels + level, 8 : cells + 8, :] = moist
        start_sum[pl.ds(level, 1), :] = jnp.sum(warm + 2.0 * moist, axis=0, keepdims=True)
        return carry

    lax.fori_loop(0, levels, spread, 0, unroll=2)
    starts, starts_in = peers(
        "narrow", lambda target: start_sum, lambda origin: start_sums.at[origin],
        start_send, start_recv,
    )
    for copy in starts:
        copy.start()
    start_sums[depth] = start_sum[...]

    courant_copy.wait()
    cloud_copy.wait()
    courant = courant_ref[...]
    left_gain[...] = (courant + 0.15) * (1.0 / 0.15)
    middle_gain[...] = (0.7 - courant) * (1.0 / 0.15)
    keep[...] = 1.0 - 0.3 * cloud_ref[...].astype(jnp.float32)

    first = me * columns
    slots = slots_ref[...]
    ranks[...] = ranked((slots >= first) & (slots < first + columns))
    slot_number = lax.broadcasted_iota(jnp.int32, (columns, columns), 0) + first
    for origin in range(wide):
        hit = (ranks[origin : origin + 1, :] == within).astype(jnp.float32).astype(bf16)
        spot = (slots_ref[origin : origin + 1, :] == slot_number).astype(jnp.float32)
        place[origin * rows : (origin + 1) * rows, :] = lax.dot_general(
            hit,
            spot.astype(bf16),
            (((1,), (1,)), ((), ())),
            preferred_element_type=jnp.float32,
        ).astype(bf16)
    down_copy.wait()
    for copy in states_in:
        copy.wait_recv()
    by_slot = lax.dot_general(
        landed[...], place[...], (((0,), (0,)), ((), ())), preferred_element_type=jnp.float32
    )
    span = by_slot.shape[0] // 2
    warm_force, moist_force = [
        jnp.dot(
            down_ref[...],
            by_slot[field * span : (field + 1) * span],
            precision=EXACT,
            preferred_element_type=jnp.float32,
        )
        for field in range(2)
    ]
    sum_force = warm_force + 2.0 * moist_force
    source_term[...] = (0.25 * cells * narrow) * sum_force
    for substep in range(SUB):
        gain = 0.25 / SCALE ** (substep + 1)
        push[2 * substep + 1] = gain * moist_force
        push[2 * substep] = gain * sum_force

    def surround(field):
        def insert(group, carry):
            at = pl.ds(pl.multiple_of(group * 16, 16), 16)
            low = low_in[field, at, :].astype(jnp.float32)
            high = high_in[field, at, :].astype(jnp.float32)
            for step in range(4):
                level = group * 4 + step
                from_row = 8 * (step // 2)
                low_part = low[from_row : from_row + 8]
                high_part = high[from_row : from_row + 8]
                if step % 2 == 0:
                    low_part = pltpu.roll(low_part, 4, 0)
                else:
                    high_part = pltpu.roll(high_part, 4, 0)
                slab[field * levels + level, 0:8, :] = low_part
                slab[field * levels + level, cells + 8 : cells + 16, :] = high_part
            return carry

        lax.fori_loop(0, levels // 4, insert, 0)

    def strided(field, level, part):
        return slab[field * levels + level, pl.ds(4 + part, 8, stride=parts), :]

    def advance(field, substep):
        last = substep == SUB - 1

        def fetch(level):
            if substep > 0:
                return [state[field * levels + level, part] for part in range(parts)]
            cell = [strided(field, level, part) for part in range(parts)]
            if field == 1:
                return cell
            return [cell[part] + 2.0 * keep_moist(level, part) for part in range(parts)]

        def across(level):
            cell = fetch(level)
            gain_left = left_gain[pl.ds(level, 1), :]
            gain_middle = middle_gain[pl.ds(level, 1), :]
            behind = [pltpu.roll(cell[-1], 1, 0)] + cell[:-1]
            ahead = cell[1:] + [pltpu.roll(cell[0], 7, 0)]
            return [
                ahead[part] + gain_left * behind[part] + gain_middle * cell[part]
                for part in range(parts)
            ]

        def finish(level, below, here, above):
            forced = push[2 * substep + field, pl.ds(level, 1), :]
            kept = keep[pl.ds(level, 1), :]
            for part in range(parts):
                value = (below[part] + above[part]) + (8.0 * here[part] + forced)
                if field == 1:
                    value = jnp.minimum(value, kept * value)
                if not last:
                    state[field * levels + level, part] = value
                    continue
                value = value * (SCALE**SUB)
                if field == 1:
                    state[levels + level, part] = value
                    slab[2 * levels + level, pl.ds(4 + part, 8, stride=parts), :] = value
                else:
                    value = value - 2.0 * state[levels + level, part]
                    slab[level, pl.ds(4 + part, 8, stride=parts), :] = value

        def climb(level, carry):
            below, here = carry
            above = across(level + 1)
            finish(level, below, here, above)
            return here, above

        bottom = across(0)
        second = across(1)
        finish(0, bottom, bottom, second)
        below, here = lax.fori_loop(1, levels - 1, climb, (bottom, second), unroll=2)
        finish(levels - 1, below, here, here)

    def keep_moist(level, part):
        return strided(1, level, part)

    for copy in moist_halo:
        copy.wait_recv()
    surround(1)
    for substep in range(SUB):
        advance(1, substep)

    def close_moist(level, carry):
        final = slab[2 * levels + level, 8 : cells + 8, :]
        out_ref[1, level] = final.astype(bf16)
        moved = final - slab[levels + level, 8 : cells + 8, :]
        moist_sum[pl.ds(level, 1), :] = jnp.sum(moved, axis=0, keepdims=True)
        return carry

    lax.fori_loop(0, levels, close_moist, 0, unroll=2)
    moist_out = pltpu.make_async_copy(out_ref.at[1], out_hbm.at[1], local_sem.at[len(pairs)])
    warm_out = pltpu.make_async_copy(out_ref.at[0], out_hbm.at[0], local_sem.at[len(pairs) + 1])
    moist_out.start()
    moists, moists_in = peers(
        "narrow", lambda target: moist_sum, lambda origin: moist_sums.at[origin],
        moist_send, moist_recv,
    )
    for copy in moists:
        copy.start()
    moist_sums[depth] = moist_sum[...]

    for copy in warm_halo:
        copy.wait_recv()
    surround(0)
    for substep in range(SUB - 1):
        advance(0, substep)

    for copy in starts_in + moists_in:
        copy.wait_recv()
    total, moist_change = start_sums[0], moist_sums[0]
    for origin in range(1, narrow):
        total = total + start_sums[origin]
        moist_change = moist_change + moist_sums[origin]
    sum_change = jnp.zeros_like(total)
    for substep in range(SUB):
        over = jnp.concatenate([total[1:], total[-1:]], axis=0)
        under = jnp.concatenate([total[:1], total[:-1]], axis=0)
        rise = 0.1 * (over - 2.0 * total + under) + source_term[...]
        total = total + rise
        sum_change = sum_change + rise
    up_copy.wait()
    changes = (sum_change - 2.0 * moist_change, moist_change)
    tendency = jnp.concatenate(
        [
            lax.dot_general(
                up_ref[...],
                change,
                (((0,), (0,)), ((), ())),
                precision=EXACT,
                preferred_element_type=jnp.float32,
            )
            for change in changes
        ],
        axis=0,
    )
    tendency = (tendency * (1.0 / (cells * narrow * SUB))).astype(bf16)
    packed_back[...] = lax.dot_general(
        place[...], tendency, (((1,), (1,)), ((), ())), preferred_element_type=jnp.float32
    ).astype(bf16)
    back, back_in = peers(
        "wide",
        lambda target: on_rows(packed_back, target * rows, rows),
        lambda origin: on_rows(landed_back, origin * rows, rows),
        back_send,
        back_recv,
    )
    for copy in back:
        copy.start()
    landed_back[own_rows, :] = packed_back[own_rows, :]

    advance(0, SUB - 1)

    def close_warm(level, carry):
        out_ref[0, level] = slab[level, 8 : cells + 8, :].astype(bf16)
        return carry

    lax.fori_loop(0, levels, close_warm, 0, unroll=2)
    warm_out.start()
    for copy in back_in:
        copy.wait_recv()
    tendency_ref[...] = lax.dot_general(
        landed_back[...], pick[...], (((0,), (0,)), ((), ())), preferred_element_type=jnp.float32
    ).astype(bf16)
    for copy in [*moist_halo, *states, *warm_halo, *starts, *moists, *back]:
        copy.wait_send()
    moist_out.wait()
    warm_out.wait()


def shards(gcm_state, crm_state, courant, cloud_mask, level_down, level_up, column_map):
    wide = lax.axis_size("wide")
    narrow = lax.axis_size("narrow")
    columns, width = gcm_state.shape
    _, levels, cells, _ = crm_state.shape
    capacity = -(-2 * columns // wide)
    rows = -(-capacity // 16) * 16
    total = wide * rows
    operands = (
        column_map.reshape(wide, columns),
        gcm_state.T,
        level_down,
        level_up.T,
        courant,
        cloud_mask,
        crm_state,
    )
    vmem = pl.BlockSpec(memory_space=pltpu.VMEM)
    hbm = pl.BlockSpec(memory_space=pltpu.HBM)
    dma = pltpu.SemaphoreType.DMA
    parts = (cells + 2 * SUB) // 8

    def held(*shape, dtype=jnp.float32):
        return pltpu.VMEM(shape, dtype)

    halo = held(2, levels * SUB, columns, dtype=jnp.bfloat16)
    routed = held(total, columns, dtype=jnp.bfloat16)
    message = held(total, width, dtype=jnp.bfloat16)
    tendency, crm_new = pl.pallas_call(
        step_kernel,
        out_shape=(
            jax.ShapeDtypeStruct((width, columns), jnp.bfloat16),
            jax.ShapeDtypeStruct(crm_state.shape, jnp.bfloat16),
        ),
        in_specs=[hbm] * len(operands),
        out_specs=(vmem, hbm),
        scratch_shapes=[
            held(*crm_state.shape, dtype=jnp.bfloat16),
            *(held(*operand.shape, dtype=operand.dtype) for operand in operands),
            *[halo] * 4,
            *[routed] * 2,
            *[message] * 4,
            held(wide, columns),
            held(3 * levels, cells + 16, columns),
            held(2 * levels, parts, 8, columns),
            *[held(levels, columns)] * 3,
            held(2 * SUB, levels, columns),
            held(levels, columns),
            held(levels, columns),
            held(narrow, levels, columns),
            held(levels, columns),
            held(narrow, levels, columns),
            dma((len(operands) + 3,)),
            *[dma((wide,))] * 4,
            *[dma((4,))] * 2,
            *[dma((narrow,))] * 4,
        ],
        compiler_params=pltpu.CompilerParams(
            collective_id=0, has_side_effects=True, vmem_limit_bytes=60 * 2**20
        ),
        name="step",
    )(*operands)
    return tendency.T, crm_new


def solution(mesh):
    placed = (
        P("wide", None),
        P(None, None, "narrow", "wide"),
        P(None, "wide"),
        P(None, "wide"),
        P(),
        P(),
        P(),
    )
    return jax.shard_map(
        shards,
        mesh=mesh,
        in_specs=placed,
        out_specs=(P("wide", None), P(None, None, "narrow", "wide")),
        check_vma=False,
    )
```
